32 devices in a mesh: req: 8 (over z, y), tp: 4 (over x, core).
Axes of the slice: x: 2, y: 2, z: 4, core: 2. Of those that a mesh axis runs over, the one named last changes fastest.
Arguments:
- tokens: bfloat16 [1024, 4096], P(('req', 'tp')), parts along dimension 0, may hold values from -400 to 400
- norm_gain: bfloat16 [4096], replicated, may hold values from 0.099609375 to 1.8984375
- qkv_weight: bfloat16 [4096, 1536], P(None, 'tp'), may hold values from -0.46875 to 0.46875
- out_weight: bfloat16 [512, 4096], P('tp'), may hold values from -0.5 to 0.5
- segment_ids: int32 [1024], P('req'), parts along dimension 0, may hold values from 0 to 7, never falling along the last dimension, each value on 1 to 42 neighbouring positions
- prefix_pages: int32 [64], P('req'), parts along dimension 0, may hold values from 1 to 16, 48 in all
- page_order: int32 [384], P('req'), parts along dimension 0, may hold values from 0 to 47, each once
- fresh_order: int32 [128], P('req'), parts along dimension 0, may hold values from 0 to 15, each once
- cache_pool: bfloat16 [2, 4, 384, 16, 128], P(None, 'tp', 'req'), parts along dimension 2, may hold values from -6 to 6
Outputs:
- attn_out: bfloat16 [1024, 4096], P(('req', 'tp')), parts along dimension 0
- fresh_pages: bfloat16 [2, 4, 128, 16, 128], P(None, 'tp', 'req'), parts along dimension 2
The draws below stay inside these ranges and needn't reach their ends.
There are 8 independent parts, one for each index of `req`. The reference program is written for one: setup_inputs(seed, part) draws one part's arguments, and reference() takes and returns one part's arrays. A program takes and returns all parts, laid end to end along the dimension named above; an argument that names none is the same for every part. Nothing has to cross between parts.
Inputs may be any that keep to these rules, and one draw needn't show every extreme that they name: `segment_ids`: segment numbers never fall; every prompt has at least one new token and one has exactly 42. `prefix_pages`: they sum to 48; the largest is 16. `page_order`: every page once. `fresh_order`: every page once.
All inputs are finite; a program needn't handle non-finite values.
Results may differ from the reference program's by a relative error of at most 0.014.
Values may be sent and summed in bfloat16 or wider, within the bound.
A program may use at most 64 MiB of HBM per device.

```python
import math
import jax
import jax.numpy as jnp
import numpy as np
from jax import lax

D = 4096
HEAD_SIZE = 128
MODEL_HEADS = 32
HEAD_DEV = 1
SEQS = 8
PAGE_LEN = 16
CACHE_PAGES = 48
HEADS = 4
TOKENS = 128
MAXP = 16
SEG_MOST = 42
FRESH_PAGES = 16
N_TP = 4


def draw_tokens(key, part):
    keys_all = jax.random.split(key, 3)
    row_scale = jnp.exp(jax.random.uniform(keys_all[0], (TOKENS // 2, 1), jnp.float32) * jnp.log(10.0))
    row_scale = jnp.repeat(row_scale, 2, axis=0)
    col_scale = jnp.exp(jax.random.uniform(keys_all[1], (1, D), jnp.float32) * jnp.log(10.0))
    paired = jax.random.normal(keys_all[2], (TOKENS, D), jnp.float32)
    return (jnp.clip(paired, -4.0, 4.0) * row_scale * col_scale).astype(jnp.bfloat16)


def draw_qkv_weight(key, part):
    keys_all = jax.random.split(key, 1)
    stacked = jnp.clip(jax.random.normal(keys_all[0], (D, HEADS, 3, HEAD_SIZE), jnp.float32), -5.0, 5.0)
    return (stacked * D ** (-0.5)).reshape(D, HEADS * 3 * HEAD_SIZE).astype(jnp.bfloat16)


def levels(key, shape, shards, low, largest):
    level = 1.0
    for dim, blocks in shards:
        heights = jax.random.uniform(jax.random.fold_in(jax.random.fold_in(key, 6), dim), (blocks,), jnp.float32, low / len(shards), largest / len(shards))
        level = level * jnp.repeat(jnp.exp(heights), shape[dim] // blocks).reshape((-1,) + (1,) * (len(shape) - 1 - dim))
    return level


def split_up(amount, total, most, slope):
    portions = [(1 << 20) // math.isqrt(grade ** slope) + 1 for grade in range(2, amount + 1)]
    surplus, holding = total - most - (amount - 1), [1] * (amount - 1)
    while surplus > 0:
        free = [i for i in range(amount - 1) if holding[i] < most]
        whole, left = sum([portions[i] for i in free]), surplus
        for i in free:
            extra = min(most - holding[i], max(1, left * portions[i] // whole), surplus)
            holding[i] = holding[i] + extra
            surplus = surplus - extra
    return np.array([most] + holding)


def uneven(key, amount, total, reach, lean):
    if amount == 2:
        one = jax.random.randint(key, (), max(1, total - reach), min(reach, total - 1) + 1)
        return jnp.stack([one, total - one])
    lengths = jnp.asarray(split_up(amount, total, reach, lean), jnp.int32)
    pairs = (amount - 1) // 2
    giver, taker = lengths[1:1 + 2 * pairs:2], lengths[2:2 + 2 * pairs:2]
    room = jnp.minimum(giver - 1, reach - taker)
    moved = jax.random.randint(jax.random.fold_in(key, 1), (pairs,), 0, 1 << 20) % (room + 1)
    lengths = lengths.at[1:1 + 2 * pairs:2].set(giver - moved).at[2:2 + 2 * pairs:2].set(taker + moved)
    return lengths[jax.random.permutation(jax.random.fold_in(key, 2), amount)]


def bell_draw(key, extent, scale, limit, shards=(), held_as=jnp.bfloat16):
    level = levels(key, extent, shards, -0.22, 0.18) if shards else 1.0
    result = jax.random.normal(key, extent, jnp.float32) * scale * level
    return jnp.minimum(jnp.maximum(result, -limit), limit).astype(held_as)


def setup_inputs(seed: int = 0, part: int = 0) -> dict:
    key_list = jax.random.split(jax.random.key(seed), 10)
    part_keys = jax.random.split(jax.random.fold_in(key_list[9], part), 10)
    tokens = draw_tokens(jax.random.fold_in(jax.random.fold_in(key_list[9], part), 71), part)
    norm_gain = jnp.clip(1.0 + 0.18 * jax.random.normal(key_list[1], (D,), jnp.float32), 0.099609375, 1.8984375).astype(jnp.bfloat16)
    qkv_weight = draw_qkv_weight(jax.random.fold_in(key_list[9], 71), part)
    out_weight = bell_draw(key_list[3], (HEADS * HEAD_SIZE, D), HEAD_SIZE ** -0.5, 0.5, ((0, 4),))
    segment_ids = jnp.searchsorted(jnp.cumsum(uneven(part_keys[4], SEQS, TOKENS, SEG_MOST, 2)), jnp.arange(TOKENS), side="right").astype(jnp.int32)
    prefix_pages = uneven(part_keys[5], SEQS, CACHE_PAGES, MAXP, 2).astype(jnp.int32)
    page_order = jax.random.permutation(part_keys[6], CACHE_PAGES).astype(jnp.int32)
    fresh_order = jax.random.permutation(part_keys[7], FRESH_PAGES).astype(jnp.int32)
    cache_pool = bell_draw(part_keys[8], (2, HEADS, CACHE_PAGES, PAGE_LEN, HEAD_SIZE), 1.0, 6.0, ((1, 4),))
    return dict(tokens=tokens, norm_gain=norm_gain, qkv_weight=qkv_weight, out_weight=out_weight, segment_ids=segment_ids, prefix_pages=prefix_pages, page_order=page_order, fresh_order=fresh_order, cache_pool=cache_pool)


def layer_norm(values, gain):
    values = values.astype(jnp.float32)
    center = values - lax.optimization_barrier(jnp.mean(values, axis=-1, keepdims=True))
    spread = lax.optimization_barrier(jnp.mean(center * center, axis=-1, keepdims=True))
    return (center * lax.rsqrt(spread + 1e-05) * gain.astype(jnp.float32)).astype(jnp.bfloat16)

def token_layout(segment_ids, prefix_pages, page_order, fresh_order, page_len):
    seq_count = prefix_pages.shape[0]
    tok_count = segment_ids.shape[0]
    labels = jnp.arange(seq_count, dtype=jnp.int32)
    member = (segment_ids[:, None] == labels[None, :]).astype(jnp.int32)
    counts = lax.optimization_barrier(jnp.sum(member, axis=0)).astype(jnp.int32)
    starts = (jnp.cumsum(counts) - counts).astype(jnp.int32)
    token_index = jnp.arange(tok_count, dtype=jnp.int32)
    in_prompt = (token_index - lax.optimization_barrier(jnp.sum(member * starts[None, :], axis=1))).astype(jnp.int32)
    prefix_len = prefix_pages * page_len
    position = (in_prompt + lax.optimization_barrier(jnp.sum(member * prefix_len[None, :], axis=1))).astype(jnp.int32)
    fresh_counts = (counts + page_len - 1) // page_len
    fresh_starts = (jnp.cumsum(fresh_counts) - fresh_counts).astype(jnp.int32)
    page_slot = (lax.optimization_barrier(jnp.sum(member * fresh_starts[None, :], axis=1)) + in_prompt // page_len).astype(jnp.int32)
    target = (jnp.take(fresh_order, page_slot) * page_len + in_prompt % page_len).astype(jnp.int32)
    page_count = page_order.shape[0]
    cache_starts = (jnp.cumsum(prefix_pages) - prefix_pages).astype(jnp.int32)
    logical = jnp.zeros((page_count,), jnp.int32).at[page_order].set(jnp.arange(page_count, dtype=jnp.int32))
    holder = (lax.optimization_barrier(jnp.sum((logical[:, None] >= cache_starts[None, :]).astype(jnp.int32), axis=1)) - 1).astype(jnp.int32)
    holder_start = lax.optimization_barrier(jnp.sum((holder[:, None] == labels[None, :]).astype(jnp.int32) * cache_starts[None, :], axis=1)).astype(jnp.int32)
    slot_index = jnp.arange(page_len, dtype=jnp.int32)
    key_owner = jnp.repeat(holder, page_len)
    key_pos = ((logical - holder_start)[:, None] * page_len + slot_index[None, :]).reshape(-1).astype(jnp.int32)
    return (in_prompt, position, target, key_owner, key_pos)

def attention_mask(segment_ids, in_prompt, position, key_owner, key_pos):
    cache_ok = segment_ids[:, None] == key_owner[None, :]
    new_ok = (segment_ids[:, None] == segment_ids[None, :]) & (in_prompt[None, :] <= in_prompt[:, None])
    allowed = jnp.concatenate([cache_ok, new_ok], axis=1)
    key_all = jnp.concatenate([key_pos, position])
    distance = (position[:, None] - key_all[None, :]).astype(jnp.float32)
    return (allowed, distance)

def attend_head(queries, key_rows, values, alibi_slope, allowed, distance):
    scores = lax.dot_general(queries, key_rows, (((1,), (1,)), ((), ())), preferred_element_type=jnp.float32)
    scores = scores * queries.shape[1] ** (-0.5) - alibi_slope * distance
    scores = jnp.where(allowed, scores, -1e+30)
    peak_score = lax.optimization_barrier(jnp.max(scores, axis=1, keepdims=True))
    weights = jnp.exp(scores - peak_score)
    weights_bf = (weights / lax.optimization_barrier(jnp.sum(weights, axis=1, keepdims=True))).astype(jnp.bfloat16)
    return jnp.dot(weights_bf, values, preferred_element_type=jnp.float32).astype(jnp.bfloat16)

def reference(tokens, norm_gain, qkv_weight, out_weight, segment_ids, prefix_pages, page_order, fresh_order, cache_pool):
    normed = layer_norm(tokens, norm_gain)
    projected = jnp.dot(normed, qkv_weight, preferred_element_type=jnp.float32).astype(jnp.bfloat16)
    in_prompt, position, target, key_owner, key_pos = token_layout(segment_ids, prefix_pages, page_order, fresh_order, PAGE_LEN)
    allowed, distance = attention_mask(segment_ids, in_prompt, position, key_owner, key_pos)
    per_head = projected.reshape(TOKENS, HEADS, 3, HEAD_SIZE).transpose(1, 2, 0, 3)
    step_heads = MODEL_HEADS // HEADS
    slopes = jnp.exp2(-8.0 * (jnp.arange(HEADS, dtype=jnp.float32) + 1.0) * step_heads / MODEL_HEADS)
    cache_flat = cache_pool.reshape(2, HEADS, CACHE_PAGES * PAGE_LEN, HEAD_SIZE).transpose(1, 0, 2, 3)

    def one_head(inputs):
        head_block, cached, alibi_slope = inputs
        key_rows = jnp.concatenate([cached[0], head_block[1]], axis=0)
        values = jnp.concatenate([cached[1], head_block[2]], axis=0)
        return attend_head(head_block[0], key_rows, values, alibi_slope, allowed, distance)
    context = lax.map(one_head, (per_head, cache_flat, slopes))
    groups = context.reshape(N_TP, HEAD_DEV, TOKENS, HEAD_SIZE).transpose(0, 2, 1, 3).reshape(N_TP, TOKENS, HEAD_DEV * HEAD_SIZE)
    weight_groups = out_weight.reshape(N_TP, HEAD_DEV * HEAD_SIZE, D)

    def add_group(running, inputs):
        group_ctx, weight = inputs
        rounded = jnp.dot(group_ctx, weight, preferred_element_type=jnp.float32).astype(jnp.bfloat16)
        rounded = lax.optimization_barrier(rounded)
        return (running + rounded.astype(jnp.float32), None)
    running, unused = lax.scan(add_group, jnp.zeros((TOKENS, D), jnp.float32), (groups, weight_groups))
    attn_out = running.astype(jnp.bfloat16)
    new_kv = per_head[:, 1:3].transpose(1, 0, 2, 3)
    fresh_pages = jnp.zeros((2, HEADS, FRESH_PAGES * PAGE_LEN, HEAD_SIZE), jnp.bfloat16).at[:, :, target].set(new_kv)
    return (attn_out, fresh_pages.reshape(2, HEADS, FRESH_PAGES, PAGE_LEN, HEAD_SIZE))
```

```python
import functools
import jax
import jax.numpy as jnp
from jax import lax
from jax.experimental import pallas as pl
from jax.experimental.pallas import tpu as pltpu
from jax.sharding import PartitionSpec as P

MODEL_HEADS = 32
K_PARTS = 8
N_PARTS = 8
F32 = jnp.float32
BF16 = jnp.bfloat16


def iota(shape, dim):
    return lax.broadcasted_iota(jnp.int32, shape, dim).astype(F32)


def to_col(row):
    size = row.shape[1]
    eye = iota((size, size), 0) == iota((size, size), 1)
    return jnp.sum(jnp.where(eye, row, 0.0), axis=1, keepdims=True)


def kernel(
    n,
    page_len,
    tok_ref,
    gain_ref,
    seg_ref,
    prefix_ref,
    order_ref,
    fresh_ref,
    w_hbm,
    wo_hbm,
    cache_hbm,
    out_ref,
    pages_ref,
    xg,
    w_v,
    wo_v,
    cache_v,
    bias_c,
    bias_n,
    ctx_own,
    ctx_sib,
    stage,
    land,
    own_sum,
    w_sem,
    wo_sem,
    cache_sem,
    cross_send,
    cross_recv,
    sib_send,
    sib_recv,
    wo_send,
    wo_recv,
    ctx_send,
    ctx_recv,
    sum_send,
    sum_recv,
):
    m = n // 2
    me = lax.axis_index("tp")
    chip, core = me // 2, lax.rem(me, 2)
    sibling = chip * 2 + (1 - core)
    rows, width = tok_ref.shape
    toks = n * rows
    head = wo_hbm.shape[0]
    kc, nc = width // K_PARTS, width // N_PARTS

    def peer(d):
        return lax.rem(chip + d, m) * 2 + core

    def at_rows(owner):
        return pl.ds(pl.multiple_of(owner * rows, rows), rows)

    cache_copy = pltpu.make_async_copy(cache_hbm, cache_v, cache_sem)
    wo_copy = pltpu.make_async_copy(wo_hbm, wo_v.at[pl.ds(0, head)], wo_sem)
    w_copies = [
        pltpu.make_async_copy(
            w_hbm.at[pl.ds(j * kc, kc)], w_v.at[pl.ds(j * kc, kc)], w_sem.at[j]
        )
        for j in range(K_PARTS)
    ]

    def cross(j, d):
        block = xg.at[j, at_rows(me)]
        return pltpu.make_async_remote_copy(
            src_ref=block,
            dst_ref=block,
            send_sem=cross_send.at[j, d - 1],
            recv_sem=cross_recv.at[j, d - 1],
            device_id={"tp": peer(d)},
            device_id_type=pl.DeviceIdType.MESH,
        )

    def forward(j, d):
        block = xg.at[j, at_rows(peer(m - d))]
        return pltpu.make_async_remote_copy(
            src_ref=block,
            dst_ref=block,
            send_sem=sib_send.at[j, d],
            recv_sem=sib_recv.at[j, d],
            device_id={"tp": sibling},
            device_id_type=pl.DeviceIdType.MESH,
        )

    wo_push = pltpu.make_async_remote_copy(
        src_ref=wo_hbm,
        dst_ref=wo_v.at[pl.ds(head, head)],
        send_sem=wo_send,
        recv_sem=wo_recv,
        device_id={"tp": sibling},
        device_id_type=pl.DeviceIdType.MESH,
    )
    ctx_push = pltpu.make_async_remote_copy(
        src_ref=ctx_own,
        dst_ref=ctx_sib,
        send_sem=ctx_send,
        recv_sem=ctx_recv,
        device_id={"tp": sibling},
        device_id_type=pl.DeviceIdType.MESH,
    )

    def give(j, d):
        return pltpu.make_async_remote_copy(
            src_ref=stage.at[d - 1, j],
            dst_ref=land.at[d - 1, j],
            send_sem=sum_send.at[d - 1, j],
            recv_sem=sum_recv.at[d - 1, j],
            device_id={"tp": peer(d)},
            device_id_type=pl.DeviceIdType.MESH,
        )

    barrier = pltpu.get_barrier_semaphore()
    for other in [sibling] + [peer(d) for d in range(1, m)]:
        pl.semaphore_signal(
            barrier, inc=1, device_id={"tp": other}, device_id_type=pl.DeviceIdType.MESH
        )
    for copy in w_copies:
        copy.start()
    cache_copy.start()
    wo_copy.start()

    values = tok_ref[...].astype(F32)
    mean = jnp.sum(values, axis=1, keepdims=True) * (1.0 / width)
    center = values - mean
    spread = jnp.sum(center * center, axis=1, keepdims=True) * (1.0 / width)
    scale = lax.rsqrt(spread + 1e-05)
    pl.semaphore_wait(barrier, m)
    for j in range(K_PARTS):
        part = slice(j * kc, (j + 1) * kc)
        piece = (tok_ref[:, part].astype(F32) - mean) * scale * gain_ref[:, part].astype(F32)
        xg[j, at_rows(me), :] = piece.astype(BF16)
        for d in range(1, m):
            cross(j, d).start()
        forward(j, 0).start()
    wo_push.start()

    seqs = prefix_ref.shape[1]
    seg_row = seg_ref[...].astype(F32)
    prefix_row = prefix_ref[...].astype(F32)
    labels = iota((seqs, toks), 0)
    member = labels == seg_row
    before = labels < seg_row
    counts = jnp.sum(jnp.where(member, 1.0, 0.0), axis=1, keepdims=True)
    starts = jnp.sum(jnp.where(before, counts, 0.0), axis=0, keepdims=True)
    inside = iota((1, toks), 1) - starts
    page_inside = jnp.floor((inside + 0.5) * (1.0 / page_len))
    fresh_counts = jnp.floor((counts + (page_len - 0.5)) * (1.0 / page_len))
    page_slot = jnp.sum(jnp.where(before, fresh_counts, 0.0), axis=0, keepdims=True) + page_inside
    fresh_col = to_col(fresh_ref[...].astype(F32))
    fresh_total = fresh_col.shape[0]
    target = jnp.sum(
        jnp.where(iota((fresh_total, toks), 0) == page_slot, fresh_col, 0.0), axis=0, keepdims=True
    )
    target = target * page_len + (inside - page_inside * page_len)
    prefix_col = to_col(prefix_row)
    pos_row = inside + page_len * jnp.sum(
        jnp.where(member, prefix_col, 0.0), axis=0, keepdims=True
    )
    seg_col = to_col(seg_row)
    pos_col = to_col(pos_row)
    cache_starts = jnp.sum(
        jnp.where(iota((seqs, seqs), 1) < iota((seqs, seqs), 0), prefix_row, 0.0),
        axis=1,
        keepdims=True,
    )
    order_col = to_col(order_ref[...].astype(F32))
    pages = order_col.shape[0]
    cached = pages * page_len
    slot = iota((1, cached), 1)
    page_id = jnp.floor((slot + 0.5) * (1.0 / page_len))
    logical = jnp.sum(
        jnp.where(order_col == page_id, iota((pages, cached), 0), 0.0), axis=0, keepdims=True
    )
    reached = logical >= cache_starts
    holder = jnp.sum(jnp.where(reached, 1.0, 0.0), axis=0, keepdims=True) - 1.0
    holder_start = jnp.max(jnp.where(reached, cache_starts, 0.0), axis=0, keepdims=True)
    key_pos = (logical - holder_start) * page_len + (slot - page_id * page_len)
    step_heads = MODEL_HEADS // n
    slope = jnp.float32(2.0 ** (-8.0 * step_heads / MODEL_HEADS))
    for h in range(1, n):
        slope = jnp.where(me == h, jnp.float32(2.0 ** (-8.0 * (h + 1) * step_heads / MODEL_HEADS)), slope)
    bias_c[...] = jnp.where(seg_col == holder, (key_pos - pos_col) * slope, -1e30)
    causal = iota((toks, toks), 1) <= iota((toks, toks), 0)
    bias_n[...] = jnp.where((seg_col == seg_row) & causal, (pos_row - pos_col) * slope, -1e30)

    def project(j, total):
        for d in range(m):
            forward(j, d).wait_recv()
        w_copies[j].wait()
        product = jnp.dot(xg[j], w_v[pl.ds(j * kc, kc), :], preferred_element_type=F32)
        return product if total is None else total + product

    total = None
    for j in range(K_PARTS):
        for d in range(1, m):
            cross(j, d).wait_recv()
            forward(j, d).start()
        if j:
            total = project(j - 1, total)
    total = project(K_PARTS - 1, total)
    projected = total.astype(BF16)
    queries = projected[:, :head]
    key_new = projected[:, head : 2 * head]
    value_new = projected[:, 2 * head :]

    cache_copy.wait()
    contract = (((1,), (1,)), ((), ()))
    norm = head ** (-0.5)
    score_c = lax.dot_general(queries, cache_v[0], contract, preferred_element_type=F32)
    score_n = lax.dot_general(queries, key_new, contract, preferred_element_type=F32)
    score_c = score_c * norm + bias_c[...]
    score_n = score_n * norm + bias_n[...]
    peak = jnp.maximum(
        jnp.max(score_c, axis=1, keepdims=True), jnp.max(score_n, axis=1, keepdims=True)
    )
    weight_c = jnp.exp(score_c - peak)
    weight_n = jnp.exp(score_n - peak)
    mass = jnp.sum(weight_c, axis=1, keepdims=True) + jnp.sum(weight_n, axis=1, keepdims=True)
    context = jnp.dot(weight_c.astype(BF16), cache_v[1], preferred_element_type=F32)
    context = context + jnp.dot(weight_n.astype(BF16), value_new, preferred_element_type=F32)
    ctx_own[...] = (context / mass).astype(BF16)
    ctx_push.start()

    spots = iota((fresh_total * page_len, toks), 0) == target
    placed = jnp.dot(
        jnp.where(spots, 1.0, 0.0).astype(BF16), projected[:, head:], preferred_element_type=F32
    ).astype(BF16)
    pages_ref[0] = placed[:, :head]
    pages_ref[1] = placed[:, head:]

    wo_copy.wait()
    wo_push.wait_recv()
    ctx_push.wait_recv()
    order = list(range(1, m)) + [0]
    left = jnp.concatenate(
        [
            jnp.concatenate([ctx_own[at_rows(peer(d)), :] for d in order], axis=0),
            jnp.concatenate([ctx_sib[at_rows(peer(d)), :] for d in order], axis=0),
        ],
        axis=1,
    )
    for j in range(N_PARTS):
        part = slice(j * nc, (j + 1) * nc)
        product = jnp.dot(left, wo_v[:, part], preferred_element_type=F32)
        for d in range(1, m):
            stage[d - 1, j] = product[(d - 1) * rows : d * rows].astype(BF16)
            give(j, d).start()
        own_sum[:, part] = product[(m - 1) * rows :]
    for j in range(N_PARTS):
        part = slice(j * nc, (j + 1) * nc)
        whole = own_sum[:, part]
        for d in range(1, m):
            give(j, d).wait_recv()
            whole = whole + land[d - 1, j].astype(F32)
        out_ref[:, part] = whole.astype(BF16)

    for j in range(K_PARTS):
        for d in range(1, m):
            cross(j, d).wait_send()
        for d in range(m):
            forward(j, d).wait_send()
    wo_push.wait_send()
    ctx_push.wait_send()
    for j in range(N_PARTS):
        for d in range(1, m):
            give(j, d).wait_send()


def body(
    tokens,
    norm_gain,
    qkv_weight,
    out_weight,
    segment_ids,
    prefix_pages,
    page_order,
    fresh_order,
    cache_pool,
):
    n = lax.axis_size("tp")
    m = n // 2
    rows, width = tokens.shape
    toks = n * rows
    head_dev, pages, page_len, head = cache_pool.shape[1:]
    cached = pages * page_len
    fresh_total = fresh_order.shape[0]
    vmem = pl.BlockSpec(memory_space=pltpu.VMEM)
    hbm = pl.BlockSpec(memory_space=pl.ANY)
    dma = pltpu.SemaphoreType.DMA
    kc, nc = width // K_PARTS, width // N_PARTS
    attn_out, fresh_pages = pl.pallas_call(
        functools.partial(kernel, n, page_len),
        out_shape=(
            jax.ShapeDtypeStruct((rows, width), BF16),
            jax.ShapeDtypeStruct((2, fresh_total * page_len, head), BF16),
        ),
        in_specs=[vmem] * 6 + [hbm] * 3,
        out_specs=(vmem, vmem),
        scratch_shapes=[
            pltpu.VMEM((K_PARTS, toks, kc), BF16),
            pltpu.VMEM((width, 3 * head), BF16),
            pltpu.VMEM((2 * head, width), BF16),
            pltpu.VMEM((2, cached, head), BF16),
            pltpu.VMEM((toks, cached), F32),
            pltpu.VMEM((toks, toks), F32),
            pltpu.VMEM((toks, head), BF16),
            pltpu.VMEM((toks, head), BF16),
            pltpu.VMEM((m - 1, N_PARTS, rows, nc), BF16),
            pltpu.VMEM((m - 1, N_PARTS, rows, nc), BF16),
            pltpu.VMEM((rows, width), F32),
            dma((K_PARTS,)),
            dma,
            dma,
            dma((K_PARTS, m - 1)),
            dma((K_PARTS, m - 1)),
            dma((K_PARTS, m)),
            dma((K_PARTS, m)),
            dma,
            dma,
            dma,
            dma,
            dma((m - 1, N_PARTS)),
            dma((m - 1, N_PARTS)),
        ],
        compiler_params=pltpu.CompilerParams(
            collective_id=0, has_side_effects=True, vmem_limit_bytes=56 * 1024 * 1024
        ),
    )(
        tokens,
        norm_gain.reshape(1, -1),
        segment_ids.reshape(1, -1),
        prefix_pages.reshape(1, -1),
        page_order.reshape(1, -1),
        fresh_order.reshape(1, -1),
        qkv_weight,
        out_weight,
        cache_pool.reshape(2, cached, head),
    )
    return attn_out, fresh_pages.reshape(2, head_dev, fresh_total, page_len, head)


def solution(mesh):
    placed = (
        P(("req", "tp"), None),
        P(),
        P(None, "tp"),
        P("tp", None),
        P("req"),
        P("req"),
        P("req"),
        P("req"),
        P(None, "tp", "req", None, None),
    )
    return jax.shard_map(
        body,
        mesh=mesh,
        in_specs=placed,
        out_specs=(P(("req", "tp"), None), P(None, "tp", "req", None, None)),
        check_vma=False,
    )
```

```python
import functools
import jax
import jax.numpy as jnp
from jax import lax
from jax.experimental import pallas as pl
from jax.experimental.pallas import tpu as pltpu
from jax.sharding import PartitionSpec as P

MODEL_HEADS = 32
K_PARTS = 8
N_PARTS = 8
F32 = jnp.float32
BF16 = jnp.bfloat16


def iota(shape, dim):
    return lax.broadcasted_iota(jnp.int32, shape, dim).astype(F32)


def to_col(row):
    size = row.shape[1]
    eye = iota((size, size), 0) == iota((size, size), 1)
    return jnp.sum(jnp.where(eye, row, 0.0), axis=1, keepdims=True)


def kernel(
    n,
    page_len,
    tok_hbm,
    gain_hbm,
    seg_hbm,
    prefix_hbm,
    order_hbm,
    fresh_hbm,
    w_hbm,
    wo_hbm,
    cache_hbm,
    out_ref,
    pages_ref,
    tok_ref,
    gain_ref,
    seg_ref,
    prefix_ref,
    order_ref,
    fresh_ref,
    xg,
    w_v,
    wo_v,
    cache_v,
    bias_c,
    bias_n,
    ctx_own,
    ctx_sib,
    stage,
    land,
    own_sum,
    in_sem,
    w_sem,
    wo_sem,
    cache_sem,
    cross_send,
    cross_recv,
    sib_send,
    sib_recv,
    wo_send,
    wo_recv,
    ctx_send,
    ctx_recv,
    sum_send,
    sum_recv,
):
    m = n // 2
    me = lax.axis_index("tp")
    chip, core = me // 2, lax.rem(me, 2)
    sibling = chip * 2 + (1 - core)
    rows, width = tok_ref.shape
    toks = n * rows
    head = wo_hbm.shape[0]
    kc, nc = width // K_PARTS, width // N_PARTS

    def peer(d):
        return lax.rem(chip + d, m) * 2 + core

    def at_rows(owner):
        return pl.ds(pl.multiple_of(owner * rows, rows), rows)

    small_in = [tok_hbm, gain_hbm, seg_hbm, prefix_hbm, order_hbm, fresh_hbm]
    small_v = [tok_ref, gain_ref, seg_ref, prefix_ref, order_ref, fresh_ref]
    small_copies = [
        pltpu.make_async_copy(source, target, in_sem.at[i])
        for i, (source, target) in enumerate(zip(small_in, small_v))
    ]
    cache_copy = pltpu.make_async_copy(cache_hbm, cache_v, cache_sem)
    wo_copy = pltpu.make_async_copy(wo_hbm, wo_v.at[pl.ds(0, head)], wo_sem)
    w_copies = [
        pltpu.make_async_copy(
            w_hbm.at[pl.ds(j * kc, kc)], w_v.at[pl.ds(j * kc, kc)], w_sem.at[j]
        )
        for j in range(K_PARTS)
    ]

    def cross(j, d):
        block = xg.at[j, at_rows(me)]
        return pltpu.make_async_remote_copy(
            src_ref=block,
            dst_ref=block,
            send_sem=cross_send.at[j, d - 1],
            recv_sem=cross_recv.at[j, d - 1],
            device_id={"tp": peer(d)},
            device_id_type=pl.DeviceIdType.MESH,
        )

    def forward(j, d):
        block = xg.at[j, at_rows(peer(m - d))]
        return pltpu.make_async_remote_copy(
            src_ref=block,
            dst_ref=block,
            send_sem=sib_send.at[j, d],
            recv_sem=sib_recv.at[j, d],
            device_id={"tp": sibling},
            device_id_type=pl.DeviceIdType.MESH,
        )

    wo_push = pltpu.make_async_remote_copy(
        src_ref=wo_hbm,
        dst_ref=wo_v.at[pl.ds(head, head)],
        send_sem=wo_send,
        recv_sem=wo_recv,
        device_id={"tp": sibling},
        device_id_type=pl.DeviceIdType.MESH,
    )
    ctx_push = pltpu.make_async_remote_copy(
        src_ref=ctx_own,
        dst_ref=ctx_sib,
        send_sem=ctx_send,
        recv_sem=ctx_recv,
        device_id={"tp": sibling},
        device_id_type=pl.DeviceIdType.MESH,
    )

    def give(j, d):
        return pltpu.make_async_remote_copy(
            src_ref=stage.at[d - 1, j],
            dst_ref=land.at[d - 1, j],
            send_sem=sum_send.at[d - 1, j],
            recv_sem=sum_recv.at[d - 1, j],
            device_id={"tp": peer(d)},
            device_id_type=pl.DeviceIdType.MESH,
        )

    for copy in small_copies[:2]:
        copy.start()
    barrier = pltpu.get_barrier_semaphore()
    for other in [sibling] + [peer(d) for d in range(1, m)]:
        pl.semaphore_signal(
            barrier, inc=1, device_id={"tp": other}, device_id_type=pl.DeviceIdType.MESH
        )
    for copy in w_copies + small_copies[2:]:
        copy.start()
    cache_copy.start()
    wo_copy.start()

    for copy in small_copies[:2]:
        copy.wait()
    values = tok_ref[...].astype(F32)
    mean = jnp.sum(values, axis=1, keepdims=True) * (1.0 / width)
    center = values - mean
    spread = jnp.sum(center * center, axis=1, keepdims=True) * (1.0 / width)
    scale = lax.rsqrt(spread + 1e-05)
    pl.semaphore_wait(barrier, m)
    for j in range(K_PARTS):
        part = slice(j * kc, (j + 1) * kc)
        piece = (tok_ref[:, part].astype(F32) - mean) * scale * gain_ref[part].reshape(1, kc).astype(F32)
        xg[j, at_rows(me), :] = piece.astype(BF16)
        for d in range(1, m):
            cross(j, d).start()
        forward(j, 0).start()
    wo_push.start()

    for copy in small_copies[2:]:
        copy.wait()
    seqs = prefix_ref.shape[1]
    seg_row = seg_ref[...].astype(F32)
    prefix_row = prefix_ref[...].astype(F32)
    labels = iota((seqs, toks), 0)
    member = labels == seg_row
    before = labels < seg_row
    counts = jnp.sum(jnp.where(member, 1.0, 0.0), axis=1, keepdims=True)
    starts = jnp.sum(jnp.where(before, counts, 0.0), axis=0, keepdims=True)
    inside = iota((1, toks), 1) - starts
    page_inside = jnp.floor((inside + 0.5) * (1.0 / page_len))
    fresh_counts = jnp.floor((counts + (page_len - 0.5)) * (1.0 / page_len))
    page_slot = jnp.sum(jnp.where(before, fresh_counts, 0.0), axis=0, keepdims=True) + page_inside
    fresh_col = to_col(fresh_ref[...].astype(F32))
    fresh_total = fresh_col.shape[0]
    target = jnp.sum(
        jnp.where(iota((fresh_total, toks), 0) == page_slot, fresh_col, 0.0), axis=0, keepdims=True
    )
    target = target * page_len + (inside - page_inside * page_len)
    prefix_col = to_col(prefix_row)
    pos_row = inside + page_len * jnp.sum(
        jnp.where(member, prefix_col, 0.0), axis=0, keepdims=True
    )
    seg_col = to_col(seg_row)
    pos_col = to_col(pos_row)
    cache_starts = jnp.sum(
        jnp.where(iota((seqs, seqs), 1) < iota((seqs, seqs), 0), prefix_row, 0.0),
        axis=1,
        keepdims=True,
    )
    order_col = to_col(order_ref[...].astype(F32))
    pages = order_col.shape[0]
    cached = pages * page_len
    slot = iota((1, cached), 1)
    page_id = jnp.floor((slot + 0.5) * (1.0 / page_len))
    logical = jnp.sum(
        jnp.where(order_col == page_id, iota((pages, cached), 0), 0.0), axis=0, keepdims=True
    )
    reached = logical >= cache_starts
    holder = jnp.sum(jnp.where(reached, 1.0, 0.0), axis=0, keepdims=True) - 1.0
    holder_start = jnp.max(jnp.where(reached, cache_starts, 0.0), axis=0, keepdims=True)
    key_pos = (logical - holder_start) * page_len + (slot - page_id * page_len)
    step_heads = MODEL_HEADS // n
    slope = jnp.float32(2.0 ** (-8.0 * step_heads / MODEL_HEADS))
    for h in range(1, n):
        slope = jnp.where(me == h, jnp.float32(2.0 ** (-8.0 * (h + 1) * step_heads / MODEL_HEADS)), slope)
    bias_c[...] = jnp.where(seg_col == holder, (key_pos - pos_col) * slope, -1e30)
    causal = iota((toks, toks), 1) <= iota((toks, toks), 0)
    bias_n[...] = jnp.where((seg_col == seg_row) & causal, (pos_row - pos_col) * slope, -1e30)

    def project(j, total):
        for d in range(m):
            forward(j, d).wait_recv()
        w_copies[j].wait()
        product = jnp.dot(xg[j], w_v[pl.ds(j * kc, kc), :], preferred_element_type=F32)
        return product if total is None else total + product

    total = None
    for j in range(K_PARTS):
        for d in range(1, m):
            cross(j, d).wait_recv()
            forward(j, d).start()
        if j:
            total = project(j - 1, total)
    total = project(K_PARTS - 1, total)
    projected = total.astype(BF16)
    queries = projected[:, :head]
    key_new = projected[:, head : 2 * head]
    value_new = projected[:, 2 * head :]

    cache_copy.wait()
    contract = (((1,), (1,)), ((), ()))
    norm = head ** (-0.5)
    score_c = lax.dot_general(queries, cache_v[0], contract, preferred_element_type=F32)
    score_n = lax.dot_general(queries, key_new, contract, preferred_element_type=F32)
    score_c = score_c * norm + bias_c[...]
    score_n = score_n * norm + bias_n[...]
    peak = jnp.maximum(
        jnp.max(score_c, axis=1, keepdims=True), jnp.max(score_n, axis=1, keepdims=True)
    )
    weight_c = jnp.exp(score_c - peak)
    weight_n = jnp.exp(score_n - peak)
    mass = jnp.sum(weight_c, axis=1, keepdims=True) + jnp.sum(weight_n, axis=1, keepdims=True)
    context = jnp.dot(weight_c.astype(BF16), cache_v[1], preferred_element_type=F32)
    context = context + jnp.dot(weight_n.astype(BF16), value_new, preferred_element_type=F32)
    ctx_own[...] = (context / mass).astype(BF16)
    ctx_push.start()

    spots = iota((fresh_total * page_len, toks), 0) == target
    placed = jnp.dot(
        jnp.where(spots, 1.0, 0.0).astype(BF16), projected[:, head:], preferred_element_type=F32
    ).astype(BF16)
    pages_ref[0] = placed[:, :head]
    pages_ref[1] = placed[:, head:]

    wo_copy.wait()
    wo_push.wait_recv()
    ctx_push.wait_recv()
    order = list(range(1, m)) + [0]
    left = jnp.concatenate(
        [
            jnp.concatenate([ctx_own[at_rows(peer(d)), :] for d in order], axis=0),
            jnp.concatenate([ctx_sib[at_rows(peer(d)), :] for d in order], axis=0),
        ],
        axis=1,
    )
    for j in range(N_PARTS):
        part = slice(j * nc, (j + 1) * nc)
        product = jnp.dot(left, wo_v[:, part], preferred_element_type=F32)
        for d in range(1, m):
            stage[d - 1, j] = product[(d - 1) * rows : d * rows].astype(BF16)
            give(j, d).start()
        own_sum[:, part] = product[(m - 1) * rows :]
    for j in range(N_PARTS):
        part = slice(j * nc, (j + 1) * nc)
        whole = own_sum[:, part]
        for d in range(1, m):
            give(j, d).wait_recv()
            whole = whole + land[d - 1, j].astype(F32)
        out_ref[:, part] = whole.astype(BF16)

    for j in range(K_PARTS):
        for d in range(1, m):
            cross(j, d).wait_send()
        for d in range(m):
            forward(j, d).wait_send()
    wo_push.wait_send()
    ctx_push.wait_send()
    for j in range(N_PARTS):
        for d in range(1, m):
            give(j, d).wait_send()


def body(
    tokens,
    norm_gain,
    qkv_weight,
    out_weight,
    segment_ids,
    prefix_pages,
    page_order,
    fresh_order,
    cache_pool,
):
    n = lax.axis_size("tp")
    m = n // 2
    rows, width = tokens.shape
    toks = n * rows
    head_dev, pages, page_len, head = cache_pool.shape[1:]
    cached = pages * page_len
    fresh_total = fresh_order.shape[0]
    vmem = pl.BlockSpec(memory_space=pltpu.VMEM)
    hbm = pl.BlockSpec(memory_space=pl.ANY)
    dma = pltpu.SemaphoreType.DMA
    kc, nc = width // K_PARTS, width // N_PARTS
    attn_out, fresh_pages = pl.pallas_call(
        functools.partial(kernel, n, page_len),
        out_shape=(
            pltpu.VMEM((rows, width), BF16),
            pltpu.VMEM((2, fresh_total * page_len, head), BF16),
        ),
        in_specs=[hbm] * 9,
        out_specs=(vmem, vmem),
        scratch_shapes=[
            pltpu.VMEM((rows, width), BF16),
            pltpu.VMEM((width,), BF16),
            pltpu.VMEM((1, toks), jnp.int32),
            pltpu.VMEM((1, prefix_pages.shape[0]), jnp.int32),
            pltpu.VMEM((1, pages), jnp.int32),
            pltpu.VMEM((1, fresh_total), jnp.int32),
            pltpu.VMEM((K_PARTS, toks, kc), BF16),
            pltpu.VMEM((width, 3 * head), BF16),
            pltpu.VMEM((2 * head, width), BF16),
            pltpu.VMEM((2, cached, head), BF16),
            pltpu.VMEM((toks, cached), F32),
            pltpu.VMEM((toks, toks), F32),
            pltpu.VMEM((toks, head), BF16),
            pltpu.VMEM((toks, head), BF16),
            pltpu.VMEM((m - 1, N_PARTS, rows, nc), BF16),
            pltpu.VMEM((m - 1, N_PARTS, rows, nc), BF16),
            pltpu.VMEM((rows, width), F32),
            dma((6,)),
            dma((K_PARTS,)),
            dma,
            dma,
            dma((K_PARTS, m - 1)),
            dma((K_PARTS, m - 1)),
            dma((K_PARTS, m)),
            dma((K_PARTS, m)),
            dma,
            dma,
            dma,
            dma,
            dma((m - 1, N_PARTS)),
            dma((m - 1, N_PARTS)),
        ],
        compiler_params=pltpu.CompilerParams(
            collective_id=0, has_side_effects=True, vmem_limit_bytes=56 * 1024 * 1024
        ),
    )(
        tokens,
        norm_gain,
        segment_ids.reshape(1, -1),
        prefix_pages.reshape(1, -1),
        page_order.reshape(1, -1),
        fresh_order.reshape(1, -1),
        qkv_weight,
        out_weight,
        cache_pool.reshape(2, cached, head),
    )
    return attn_out, fresh_pages.reshape(2, head_dev, fresh_total, page_len, head)


def solution(mesh):
    placed = (
        P(("req", "tp"), None),
        P(),
        P(None, "tp"),
        P("tp", None),
        P("req"),
        P("req"),
        P("req"),
        P("req"),
        P(None, "tp", "req", None, None),
    )
    return jax.shard_map(
        body,
        mesh=mesh,
        in_specs=placed,
        out_specs=(P(("req", "tp"), None), P(None, "tp", "req", None, None)),
        check_vma=False,
    )
```

```python
import functools
import jax
import jax.numpy as jnp
from jax import lax
from jax.experimental import pallas as pl
from jax.experimental.pallas import tpu as pltpu
from jax.sharding import PartitionSpec as P

MODEL_HEADS = 32
K_PARTS = 4
N_PARTS = 8
F32 = jnp.float32
BF16 = jnp.bfloat16


def iota(shape, dim):
    return lax.broadcasted_iota(jnp.int32, shape, dim).astype(F32)


def to_col(row):
    size = row.shape[1]
    eye = iota((size, size), 0) == iota((size, size), 1)
    return jnp.sum(jnp.where(eye, row, 0.0), axis=1, keepdims=True)


def kernel(
    n,
    page_len,
    tok_hbm,
    gain_hbm,
    seg_hbm,
    prefix_hbm,
    order_hbm,
    fresh_hbm,
    w_hbm,
    wo_hbm,
    cache_hbm,
    out_ref,
    pages_ref,
    tok_ref,
    gain_ref,
    seg_ref,
    prefix_ref,
    order_ref,
    fresh_ref,
    xg,
    w_v,
    wo_v,
    cache_v,
    bias_c,
    bias_n,
    ctx_own,
    ctx_sib,
    stage,
    land,
    own_sum,
    in_sem,
    w_sem,
    wo_sem,
    cache_sem,
    cross_send,
    cross_recv,
    sib_send,
    sib_recv,
    wo_send,
    wo_recv,
    ctx_send,
    ctx_recv,
    sum_send,
    sum_recv,
):
    m = n // 2
    me = lax.axis_index("tp")
    chip, core = me // 2, lax.rem(me, 2)
    sibling = chip * 2 + (1 - core)
    rows, width = tok_ref.shape
    toks = n * rows
    head = wo_hbm.shape[0]
    kc, nc = width // K_PARTS, width // N_PARTS

    def peer(d):
        return lax.rem(chip + d, m) * 2 + core

    def at_rows(owner):
        return pl.ds(pl.multiple_of(owner * rows, rows), rows)

    small_in = [tok_hbm, gain_hbm, seg_hbm, prefix_hbm, order_hbm, fresh_hbm]
    small_v = [tok_ref, gain_ref, seg_ref, prefix_ref, order_ref, fresh_ref]
    small_copies = [
        pltpu.make_async_copy(source, target, in_sem.at[i])
        for i, (source, target) in enumerate(zip(small_in, small_v))
    ]
    cache_copy = pltpu.make_async_copy(cache_hbm, cache_v, cache_sem)
    wo_copy = pltpu.make_async_copy(wo_hbm, wo_v.at[pl.ds(0, head)], wo_sem)
    w_copies = [
        pltpu.make_async_copy(
            w_hbm.at[pl.ds(j * kc, kc)], w_v.at[pl.ds(j * kc, kc)], w_sem.at[j]
        )
        for j in range(K_PARTS)
    ]

    def cross(j, d):
        block = xg.at[j, at_rows(me)]
        return pltpu.make_async_remote_copy(
            src_ref=block,
            dst_ref=block,
            send_sem=cross_send.at[j, d - 1],
            recv_sem=cross_recv.at[j, d - 1],
            device_id={"tp": peer(d)},
            device_id_type=pl.DeviceIdType.MESH,
        )

    def forward(j, d):
        block = xg.at[j, at_rows(peer(m - d))]
        return pltpu.make_async_remote_copy(
            src_ref=block,
            dst_ref=block,
            send_sem=sib_send.at[j, d],
            recv_sem=sib_recv.at[j, d],
            device_id={"tp": sibling},
            device_id_type=pl.DeviceIdType.MESH,
        )

    wo_push = pltpu.make_async_remote_copy(
        src_ref=wo_hbm,
        dst_ref=wo_v.at[pl.ds(head, head)],
        send_sem=wo_send,
        recv_sem=wo_recv,
        device_id={"tp": sibling},
        device_id_type=pl.DeviceIdType.MESH,
    )
    ctx_push = pltpu.make_async_remote_copy(
        src_ref=ctx_own,
        dst_ref=ctx_sib,
        send_sem=ctx_send,
        recv_sem=ctx_recv,
        device_id={"tp": sibling},
        device_id_type=pl.DeviceIdType.MESH,
    )

    def give(j, d):
        return pltpu.make_async_remote_copy(
            src_ref=stage.at[d - 1, j],
            dst_ref=land.at[d - 1, j],
            send_sem=sum_send.at[d - 1, j],
            recv_sem=sum_recv.at[d - 1, j],
            device_id={"tp": peer(d)},
            device_id_type=pl.DeviceIdType.MESH,
        )

    for copy in small_copies[:2]:
        copy.start()
    barrier = pltpu.get_barrier_semaphore()
    for other in [sibling] + [peer(d) for d in range(1, m)]:
        pl.semaphore_signal(
            barrier, inc=1, device_id={"tp": other}, device_id_type=pl.DeviceIdType.MESH
        )
    for copy in w_copies + small_copies[2:]:
        copy.start()
    cache_copy.start()
    wo_copy.start()

    for copy in small_copies[:2]:
        copy.wait()
    values = tok_ref[...].astype(F32)
    mean = jnp.sum(values, axis=1, keepdims=True) * (1.0 / width)
    center = values - mean
    spread = jnp.sum(center * center, axis=1, keepdims=True) * (1.0 / width)
    scale = lax.rsqrt(spread + 1e-05)
    pl.semaphore_wait(barrier, m)
    for j in range(K_PARTS):
        part = slice(j * kc, (j + 1) * kc)
        piece = (tok_ref[:, part].astype(F32) - mean) * scale * gain_ref[part].reshape(1, kc).astype(F32)
        xg[j, at_rows(me), :] = piece.astype(BF16)
        for d in range(1, m):
            cross(j, d).start()
        forward(j, 0).start()
    wo_push.start()

    for copy in small_copies[2:]:
        copy.wait()
    seqs = prefix_ref.shape[1]
    seg_row = seg_ref[...].astype(F32)
    prefix_row = prefix_ref[...].astype(F32)
    labels = iota((seqs, toks), 0)
    member = labels == seg_row
    before = labels < seg_row
    counts = jnp.sum(jnp.where(member, 1.0, 0.0), axis=1, keepdims=True)
    starts = jnp.sum(jnp.where(before, counts, 0.0), axis=0, keepdims=True)
    inside = iota((1, toks), 1) - starts
    page_inside = jnp.floor((inside + 0.5) * (1.0 / page_len))
    fresh_counts = jnp.floor((counts + (page_len - 0.5)) * (1.0 / page_len))
    page_slot = jnp.sum(jnp.where(before, fresh_counts, 0.0), axis=0, keepdims=True) + page_inside
    fresh_col = to_col(fresh_ref[...].astype(F32))
    fresh_total = fresh_col.shape[0]
    target = jnp.sum(
        jnp.where(iota((fresh_total, toks), 0) == page_slot, fresh_col, 0.0), axis=0, keepdims=True
    )
    target = target * page_len + (inside - page_inside * page_len)
    prefix_col = to_col(prefix_row)
    pos_row = inside + page_len * jnp.sum(
        jnp.where(member, prefix_col, 0.0), axis=0, keepdims=True
    )
    seg_col = to_col(seg_row)
    pos_col = to_col(pos_row)
    cache_starts = jnp.sum(
        jnp.where(iota((seqs, seqs), 1) < iota((seqs, seqs), 0), prefix_row, 0.0),
        axis=1,
        keepdims=True,
    )
    order_col = to_col(order_ref[...].astype(F32))
    pages = order_col.shape[0]
    cached = pages * page_len
    slot = iota((1, cached), 1)
    page_id = jnp.floor((slot + 0.5) * (1.0 / page_len))
    logical = jnp.sum(
        jnp.where(order_col == page_id, iota((pages, cached), 0), 0.0), axis=0, keepdims=True
    )
    reached = logical >= cache_starts
    holder = jnp.sum(jnp.where(reached, 1.0, 0.0), axis=0, keepdims=True) - 1.0
    holder_start = jnp.max(jnp.where(reached, cache_starts, 0.0), axis=0, keepdims=True)
    key_pos = (logical - holder_start) * page_len + (slot - page_id * page_len)
    step_heads = MODEL_HEADS // n
    slope = jnp.float32(2.0 ** (-8.0 * step_heads / MODEL_HEADS))
    for h in range(1, n):
        slope = jnp.where(me == h, jnp.float32(2.0 ** (-8.0 * (h + 1) * step_heads / MODEL_HEADS)), slope)
    bias_c[...] = jnp.where(seg_col == holder, (key_pos - pos_col) * slope, -1e30)
    causal = iota((toks, toks), 1) <= iota((toks, toks), 0)
    bias_n[...] = jnp.where((seg_col == seg_row) & causal, (pos_row - pos_col) * slope, -1e30)

    def project(j, total):
        for d in range(m):
            forward(j, d).wait_recv()
        w_copies[j].wait()
        product = jnp.dot(xg[j], w_v[pl.ds(j * kc, kc), :], preferred_element_type=F32)
        return product if total is None else total + product

    total = None
    for j in range(K_PARTS):
        for d in range(1, m):
            cross(j, d).wait_recv()
            forward(j, d).start()
        if j:
            total = project(j - 1, total)
    total = project(K_PARTS - 1, total)
    projected = total.astype(BF16)
    queries = projected[:, :head]
    key_new = projected[:, head : 2 * head]
    value_new = projected[:, 2 * head :]

    cache_copy.wait()
    contract = (((1,), (1,)), ((), ()))
    norm = head ** (-0.5)
    score_c = lax.dot_general(queries, cache_v[0], contract, preferred_element_type=F32)
    score_n = lax.dot_general(queries, key_new, contract, preferred_element_type=F32)
    score_c = score_c * norm + bias_c[...]
    score_n = score_n * norm + bias_n[...]
    peak = jnp.maximum(
        jnp.max(score_c, axis=1, keepdims=True), jnp.max(score_n, axis=1, keepdims=True)
    )
    weight_c = jnp.exp(score_c - peak)
    weight_n = jnp.exp(score_n - peak)
    mass = jnp.sum(weight_c, axis=1, keepdims=True) + jnp.sum(weight_n, axis=1, keepdims=True)
    context = jnp.dot(weight_c.astype(BF16), cache_v[1], preferred_element_type=F32)
    context = context + jnp.dot(weight_n.astype(BF16), value_new, preferred_element_type=F32)
    ctx_own[...] = (context / mass).astype(BF16)
    ctx_push.start()

    spots = iota((fresh_total * page_len, toks), 0) == target
    placed = jnp.dot(
        jnp.where(spots, 1.0, 0.0).astype(BF16), projected[:, head:], preferred_element_type=F32
    ).astype(BF16)
    pages_ref[0] = placed[:, :head]
    pages_ref[1] = placed[:, head:]

    wo_copy.wait()
    wo_push.wait_recv()
    ctx_push.wait_recv()
    order = list(range(1, m)) + [0]
    left = jnp.concatenate(
        [
            jnp.concatenate([ctx_own[at_rows(peer(d)), :] for d in order], axis=0),
            jnp.concatenate([ctx_sib[at_rows(peer(d)), :] for d in order], axis=0),
        ],
        axis=1,
    )
    for j in range(N_PARTS):
        part = slice(j * nc, (j + 1) * nc)
        product = jnp.dot(left, wo_v[:, part], preferred_element_type=F32)
        for d in range(1, m):
            stage[d - 1, j] = product[(d - 1) * rows : d * rows].astype(BF16)
            give(j, d).start()
        own_sum[:, part] = product[(m - 1) * rows :]
    for j in range(N_PARTS):
        part = slice(j * nc, (j + 1) * nc)
        whole = own_sum[:, part]
        for d in range(1, m):
            give(j, d).wait_recv()
            whole = whole + land[d - 1, j].astype(F32)
        out_ref[:, part] = whole.astype(BF16)

    for j in range(K_PARTS):
        for d in range(1, m):
            cross(j, d).wait_send()
        for d in range(m):
            forward(j, d).wait_send()
    wo_push.wait_send()
    ctx_push.wait_send()
    for j in range(N_PARTS):
        for d in range(1, m):
            give(j, d).wait_send()


def write_out(attn_v, pages_v, attn_hbm, pages_hbm, sem):
    copies = [
        pltpu.make_async_copy(attn_v, attn_hbm, sem.at[0]),
        pltpu.make_async_copy(pages_v, pages_hbm, sem.at[1]),
    ]
    for copy in copies:
        copy.start()
    for copy in copies:
        copy.wait()


def body(
    tokens,
    norm_gain,
    qkv_weight,
    out_weight,
    segment_ids,
    prefix_pages,
    page_order,
    fresh_order,
    cache_pool,
):
    n = lax.axis_size("tp")
    m = n // 2
    rows, width = tokens.shape
    toks = n * rows
    head_dev, pages, page_len, head = cache_pool.shape[1:]
    cached = pages * page_len
    fresh_total = fresh_order.shape[0]
    vmem = pl.BlockSpec(memory_space=pltpu.VMEM)
    hbm = pl.BlockSpec(memory_space=pl.ANY)
    dma = pltpu.SemaphoreType.DMA
    kc, nc = width // K_PARTS, width // N_PARTS
    attn_out, fresh_pages = pl.pallas_call(
        functools.partial(kernel, n, page_len),
        out_shape=(
            pltpu.VMEM((rows, width), BF16),
            pltpu.VMEM((2, fresh_total * page_len, head), BF16),
        ),
        in_specs=[hbm] * 9,
        out_specs=(vmem, vmem),
        scratch_shapes=[
            pltpu.VMEM((rows, width), BF16),
            pltpu.VMEM((width,), BF16),
            pltpu.VMEM((1, toks), jnp.int32),
            pltpu.VMEM((1, prefix_pages.shape[0]), jnp.int32),
            pltpu.VMEM((1, pages), jnp.int32),
            pltpu.VMEM((1, fresh_total), jnp.int32),
            pltpu.VMEM((K_PARTS, toks, kc), BF16),
            pltpu.VMEM((width, 3 * head), BF16),
            pltpu.VMEM((2 * head, width), BF16),
            pltpu.VMEM((2, cached, head), BF16),
            pltpu.VMEM((toks, cached), F32),
            pltpu.VMEM((toks, toks), F32),
            pltpu.VMEM((toks, head), BF16),
            pltpu.VMEM((toks, head), BF16),
            pltpu.VMEM((m - 1, N_PARTS, rows, nc), BF16),
            pltpu.VMEM((m - 1, N_PARTS, rows, nc), BF16),
            pltpu.VMEM((rows, width), F32),
            dma((6,)),
            dma((K_PARTS,)),
            dma,
            dma,
            dma((K_PARTS, m - 1)),
            dma((K_PARTS, m - 1)),
            dma((K_PARTS, m)),
            dma((K_PARTS, m)),
            dma,
            dma,
            dma,
            dma,
            dma((m - 1, N_PARTS)),
            dma((m - 1, N_PARTS)),
        ],
        compiler_params=pltpu.CompilerParams(
            collective_id=0, has_side_effects=True, vmem_limit_bytes=56 * 1024 * 1024
        ),
    )(
        tokens,
        norm_gain,
        segment_ids.reshape(1, -1),
        prefix_pages.reshape(1, -1),
        page_order.reshape(1, -1),
        fresh_order.reshape(1, -1),
        qkv_weight,
        out_weight,
        cache_pool.reshape(2, cached, head),
    )
    attn_out, fresh_pages = pl.pallas_call(
        write_out,
        out_shape=(
            jax.ShapeDtypeStruct(attn_out.shape, BF16),
            jax.ShapeDtypeStruct(fresh_pages.shape, BF16),
        ),
        in_specs=[vmem] * 2,
        out_specs=(hbm, hbm),
        scratch_shapes=[dma((2,))],
    )(
        pltpu.with_memory_space_constraint(attn_out, pltpu.VMEM),
        pltpu.with_memory_space_constraint(fresh_pages, pltpu.VMEM),
    )
    return attn_out, fresh_pages.reshape(2, head_dev, fresh_total, page_len, head)


def solution(mesh):
    placed = (
        P(("req", "tp"), None),
        P(),
        P(None, "tp"),
        P("tp", None),
        P("req"),
        P("req"),
        P("req"),
        P("req"),
        P(None, "tp", "req", None, None),
    )
    return jax.shard_map(
        body,
        mesh=mesh,
        in_specs=placed,
        out_specs=(P(("req", "tp"), None), P(None, "tp", "req", None, None)),
        check_vma=False,
    )
```
